512 devices in a mesh: group: 8 (over z), mem: 64 (over x, y, core).
Axes of the slice: x: 4, y: 8, z: 8, core: 2. Of those that a mesh axis runs over, the one named last changes fastest.
Arguments:
- node_memory: float32 [8, 16384, 512], P('group', 'mem'), may hold values from -6 to 6
- batch_owner: int32 [8, 8192, 1], P('group', 'mem'), may hold values from 0 to 63; in each aligned block of 128 rows (0 to 127, 128 to 255, ..., all dimensions but the last counted through in order) at most 4 rows name the same one
- batch_row: int32 [8, 8192], P('group', 'mem'), may hold values from 0 to 255
- batch_time: int32 [8, 8192], P('group', 'mem'), may hold values from 4096 to 8191
- neighbour_owner: int32 [8, 81920, 1], P('group', 'mem'), may hold values from 0 to 63; in each aligned block of 1280 rows (0 to 1279, 1280 to 2559, ..., all dimensions but the last counted through in order) at most 40 rows name the same one
- neighbour_row: int32 [8, 81920], P('group', 'mem'), may hold values from 0 to 255
- neighbour_time: int32 [8, 81920], P('group', 'mem'), may hold values from 0 to 4095
- frequency: float32 [512], replicated, may hold values from 0.0001 to 0.03
- phase_shift: float32 [512], replicated, may hold values from -3.140625 to 3.140625
- w_message: bfloat16 [512, 512], replicated, may hold values from -0.25 to 0.25
- w_input: bfloat16 [512, 1536], replicated, may hold values from -0.25 to 0.25
- w_recur: bfloat16 [512, 1536], replicated, may hold values from -0.25 to 0.25
- cotangent: bfloat16 [8, 8192, 512], P('group', 'mem'), may hold values from -6 to 6
Outputs:
- new_memory: float32 [8, 16384, 512], P('group', 'mem')
- grad_input: float32 [512, 1536], P('mem')
The draws below stay inside these ranges and needn't reach their ends.
Inputs may be any that keep to these rules, and one draw needn't show every extreme that they name: `batch_owner`: in each aligned block of 128 rows (the rows of one device) no owner is named by more than 4 rows, a bound that some block reaches. `neighbour_owner`: in each aligned block of 1280 rows (the rows of one device) no owner is named by more than 40 rows, a bound that some block reaches.
All inputs are finite; a program needn't handle non-finite values.
Results may differ from the reference program's by a relative error of at most 0.013.
Values may be sent and summed in bfloat16 or wider, within the bound.
A program may use at most 64 MiB of HBM per device.

```python
import math
import jax
import jax.numpy as jnp
import numpy as np
from jax import lax

M = 512
NBRS = 10
NODE_DEV = 256
BATCH_DEV = 128
GROUPS = 8
NODES = 16384
BATCH = 8192
NBR_ROWS = 81920
CAPB = 4
CAPN = 40
N_MEM = 64


def with_ends(values, key, least, high):
    longest = values.shape.index(max(values.shape))
    spots = []
    for shift in (0, 1):
        where = [jax.random.randint(jax.random.fold_in(key, axis), (), 0, length) for axis, length in enumerate(values.shape)]
        where[longest] = (where[longest] + shift) % values.shape[longest]
        spots.append(tuple(where))
    return values.at[spots[0]].set(least).at[spots[1]].set(high)


def block_levels(stream_key, shape, cuts, smallest, top_value):
    factor_of, own = 1.0, jax.random.fold_in(stream_key, 6)
    for position, parts in cuts:
        draws = jnp.exp(jax.random.uniform(jax.random.fold_in(own, position), (parts,), jnp.float32, smallest / len(cuts), top_value / len(cuts)))
        factor_of = factor_of * jnp.repeat(draws, shape[position] // parts).reshape([-1 if axis == position else 1 for axis in range(len(shape))])
    return factor_of


def assign_block(rng, own, number, rows, count, top, most, lean):
    ranking = jax.random.permutation(rng, count)
    packed, ordinary = portions_of(count, rows * top, most, lean, True), portions_of(count, rows * top, most, lean, False)
    places = jnp.arange(count)

    def named(tallies, rotation):
        used = int((tallies > 0).sum())
        fixed = max(1, used // 4)
        passed = fixed + (places - fixed + rotation * (used - fixed)) % max(1, count - fixed)
        return jnp.zeros((count,), jnp.int32).at[ranking[jnp.where(places < fixed, places, passed)]].set(jnp.asarray(tallies, jnp.int32))

    tallies = jnp.where(number % 4 == 0, named(packed, number // 4), named(ordinary, number - number // 4 - 1))
    mixed = jax.random.permutation(jax.random.fold_in(own, 3), count)
    donor, receiver = mixed[0:count // 2 * 2:2], mixed[1:count // 2 * 2:2]
    room = jnp.minimum(tallies[donor] - 1, most - tallies[receiver]) // 2
    room = jnp.where((donor == ranking[0]) | (receiver == ranking[0]) | (tallies[receiver] == 0), 0, jnp.maximum(room, 0))
    passed = jax.random.randint(jax.random.fold_in(own, 4), (count // 2,), 0, 1 << 20) % (room + 1)
    tallies = tallies.at[donor].add(-passed).at[receiver].add(passed)
    labels = jnp.searchsorted(jnp.cumsum(tallies), jnp.arange(rows * top), side="right").astype(jnp.int32)
    grid = labels.reshape(top, rows).T
    grid = grid[jax.random.permutation(jax.random.fold_in(own, 1), rows)]
    rotation = jax.random.randint(jax.random.fold_in(own, 2), (rows, 1), 0, top)
    return jnp.take_along_axis(grid, (jnp.arange(top)[None, :] + rotation) % top, axis=1)


def portions_of(amount, total, reach, slope, full):
    portions = [(1 << 20) // math.isqrt(rank ** slope) + 1 for rank in range(1, amount + 1)]
    largest = reach if full else min(reach, max(-(-total // amount), total * portions[0] // sum(portions)))
    least = 1 if total - largest >= amount - 1 else 0
    counts, surplus = [largest] + [least] * (amount - 1), total - largest - least * (amount - 1)
    while surplus > 0:
        movable = [i for i in range(1, amount) if counts[i] < largest] or [i for i in range(1, amount) if counts[i] < reach]
        mass, budget = sum([portions[i] for i in movable]), surplus
        for i in movable:
            more = min(reach - counts[i], max(1, budget * portions[i] // mass), surplus)
            counts[i] = counts[i] + more
            surplus = surplus - more
    return np.array(counts)


def gaussian(own_key, shape, width, reach, shards=(), kind=jnp.bfloat16):
    result = jax.random.normal(own_key, shape, jnp.float32) * width
    if len(shards) > 0:
        result = block_levels(own_key, shape, shards, -0.22, 0.18) * result
    return jnp.clip(result, min=-reach, max=reach).astype(kind)


def setup_inputs(seed: int = 0) -> dict:
    arg_keys = jax.random.split(jax.random.key(seed), 14)
    node_memory = gaussian(arg_keys[0], (GROUPS, NODES, M), 1.0, 6.0, ((0, 8), (1, 64)), jnp.float32)
    batch_owner_keys = jax.random.split(jax.random.fold_in(arg_keys[1], 1), GROUPS * BATCH // BATCH_DEV)
    batch_owner_turns = jax.random.permutation(jax.random.fold_in(arg_keys[1], 3), GROUPS * BATCH // BATCH_DEV)
    batch_owner = jax.vmap(lambda own, number: assign_block(jax.random.fold_in(arg_keys[1], 2), own, number, BATCH_DEV, N_MEM, 1, CAPB, 2))(batch_owner_keys, batch_owner_turns).reshape((GROUPS, BATCH, 1))
    batch_row = with_ends(jax.random.randint(arg_keys[2], (GROUPS, BATCH), 0, NODE_DEV), jax.random.fold_in(arg_keys[2], 1), 0, NODE_DEV - 1).astype(jnp.int32)
    batch_time = with_ends(jax.random.randint(arg_keys[3], (GROUPS, BATCH), 4096, 8192), jax.random.fold_in(arg_keys[3], 1), 4096, 8191).astype(jnp.int32)
    neighbour_owner_keys = jax.random.split(jax.random.fold_in(arg_keys[4], 1), GROUPS * NBR_ROWS // (BATCH_DEV * NBRS))
    neighbour_owner_turns = jax.random.permutation(jax.random.fold_in(arg_keys[4], 3), GROUPS * NBR_ROWS // (BATCH_DEV * NBRS))
    neighbour_owner = jax.vmap(lambda own, number: assign_block(jax.random.fold_in(arg_keys[4], 2), own, number, BATCH_DEV * NBRS, N_MEM, 1, CAPN, 2))(neighbour_owner_keys, neighbour_owner_turns).reshape((GROUPS, NBR_ROWS, 1))
    neighbour_row = with_ends(jax.random.randint(arg_keys[5], (GROUPS, NBR_ROWS), 0, NODE_DEV), jax.random.fold_in(arg_keys[5], 1), 0, NODE_DEV - 1).astype(jnp.int32)
    neighbour_time = with_ends(jax.random.randint(arg_keys[6], (GROUPS, NBR_ROWS), 0, 4096), jax.random.fold_in(arg_keys[6], 1), 0, 4095).astype(jnp.int32)
    frequency = jnp.clip(jnp.exp(jax.random.uniform(arg_keys[7], (M,), jnp.float32, math.log(0.0001), math.log(0.03))), 0.0001, 0.03)
    phase_shift = jnp.clip(jax.random.uniform(arg_keys[8], (M,), jnp.float32, -3.140625, 3.140625), -3.140625, 3.140625)
    w_message = gaussian(arg_keys[9], (M, M), M ** -0.5, 0.25)
    w_input = gaussian(arg_keys[10], (M, 3 * M), M ** -0.5, 0.25)
    w_recur = gaussian(arg_keys[11], (M, 3 * M), M ** -0.5, 0.25)
    cotangent = gaussian(arg_keys[12], (GROUPS, BATCH, M), 1.0, 6.0, ((0, 8), (1, 64)))
    return dict(node_memory=node_memory, batch_owner=batch_owner, batch_row=batch_row, batch_time=batch_time, neighbour_owner=neighbour_owner, neighbour_row=neighbour_row, neighbour_time=neighbour_time, frequency=frequency, phase_shift=phase_shift, w_message=w_message, w_input=w_input, w_recur=w_recur, cotangent=cotangent)


age_scale = 1024.0


def product(left, right):
    return jnp.dot(left.astype(jnp.float32), right.astype(jnp.float32), precision=lax.Precision.HIGHEST)


def encode_messages(fetched, age_vals, frequency, phase_shift, w_message):
    encoding = jnp.cos(age_vals[..., None] * frequency + phase_shift)
    inputs = (fetched + encoding).astype(jnp.bfloat16)
    return jax.nn.silu(product(inputs, w_message)).astype(jnp.bfloat16)


def aggregate(messages, age_vals, neighbours):
    weight = 1.0 / (1.0 + age_vals / age_scale)
    rows_total = messages.shape[0] // neighbours
    weighted = (messages.astype(jnp.float32) * weight[:, None]).reshape(rows_total, neighbours, -1).sum(axis=1)
    total = weight.reshape(rows_total, neighbours).sum(axis=1)
    return (weighted / total[:, None]).astype(jnp.bfloat16)


def recurrent(inputs_bf, hidden, w_input, w_recur, cotangent):
    gate_in = product(inputs_bf, w_input)
    gate_rec = product(hidden.astype(jnp.bfloat16), w_recur)
    size = hidden.shape[1]
    update_gate = jax.nn.sigmoid(gate_in[:, :size] + gate_rec[:, :size])
    reset_gate = jax.nn.sigmoid(gate_in[:, size:2 * size] + gate_rec[:, size:2 * size])
    recur_part = gate_rec[:, 2 * size:]
    candidate = jnp.tanh(gate_in[:, 2 * size:] + reset_gate * recur_part)
    hidden_new = (1.0 - update_gate) * hidden + update_gate * candidate
    upstream = cotangent.astype(jnp.float32)
    d_cand = upstream * update_gate * (1.0 - candidate * candidate)
    d_update = upstream * (candidate - hidden) * update_gate * (1.0 - update_gate)
    d_reset = d_cand * recur_part * reset_gate * (1.0 - reset_gate)
    d_pre = jnp.concatenate([d_update, d_reset, d_cand], axis=1).astype(jnp.bfloat16)
    return hidden_new, d_pre


def reference(node_memory, batch_owner, batch_row, batch_time, neighbour_owner, neighbour_row, neighbour_time, frequency, phase_shift, w_message, w_input, w_recur, cotangent):
    def group_step(group_index):
        owned = node_memory[group_index]
        batch_ids = (batch_owner[group_index, :, 0] * NODE_DEV + batch_row[group_index]).astype(jnp.int32)
        neighbour_ids = (neighbour_owner[group_index, :, 0] * NODE_DEV + neighbour_row[group_index]).astype(jnp.int32)
        age_vals = (jnp.repeat(batch_time[group_index], NBRS) - neighbour_time[group_index]).astype(jnp.float32)
        messages = encode_messages(owned[neighbour_ids], age_vals, frequency, phase_shift, w_message)
        inputs_bf = aggregate(messages, age_vals, NBRS)
        hidden = owned[batch_ids]
        hidden_new, d_pre = recurrent(inputs_bf, hidden, w_input, w_recur, cotangent[group_index])
        updated = owned.at[batch_ids].add(hidden_new - hidden)
        grads = jnp.dot(inputs_bf.astype(jnp.float32).T, d_pre.astype(jnp.float32), precision=lax.Precision.HIGHEST)
        return updated, grads

    updated, grads = lax.map(group_step, jnp.arange(GROUPS, dtype=jnp.int32))
    return updated, jnp.sum(grads, axis=0)
```

```python
import math

import jax
import jax.numpy as jnp
from jax import lax
from jax.experimental import pallas as pl
from jax.experimental.pallas import tpu as pltpu
from jax.sharding import PartitionSpec as P

f32, bf16, i32 = jnp.float32, jnp.bfloat16, jnp.int32
MESH = pl.DeviceIdType.MESH

age_scale = 1024.0
X, Y, Z = 4, 8, 8
ROW = 2 * X
WIDTH = 512
NODE = 256
BATCH = 128
NBRS = 10
CAPN, CAPB = 40, 4
SLOT = 48
BLOCK = ROW * SLOT
COS = (
    1.0,
    -19.73920440673828,
    64.93911743164062,
    -85.45014190673828,
    60.16762924194336,
    -25.967599868774414,
    6.528658390045166,
)


def inv_row(d):
    return ((-(d // 2)) % X) * 2 + d % 2


def inv_y(e):
    return (-e) % Y


def iota(shape, dim):
    return lax.broadcasted_iota(i32, shape, dim)


def mm(a, b):
    return lax.dot_general(a, b, (((1,), (0,)), ((), ())), preferred_element_type=f32)


def mm_nt(a, b):
    return lax.dot_general(a, b, (((1,), (1,)), ((), ())), preferred_element_type=f32)


def mm_tn(a, b):
    return lax.dot_general(a, b, (((0,), (0,)), ((), ())), preferred_element_type=f32)


def onehot(mask):
    return jnp.where(mask, 1.0, 0.0).astype(bf16)


def sigmoid(v):
    return 0.5 * jnp.tanh(0.5 * v) + 0.5


def kernel(
    meta, freq, phase, node_hbm, wm_hbm, wi_hbm, wr_hbm, ct_hbm,
    out_mem, out_grad,
    node, wm, wi, wr, ct, load_sem,
    coltab, y_send, y_recv,
    askbuf, askrecv, ask_send, ask_recv,
    idbuf, idrecv, id_send, id_recv,
    slotrow, slotval, encos, a_hi, a_lo, pick,
    sendbuf, slots, s_send, s_recv,
    agg, hid,
    sel, tsc, perm,
    wbs, wb1, wb2, wx_send, wx_recv, wy_send, wy_recv,
    fact, dpre, c_send, c_recv,
    gx, gxr, gx_send, gx_recv,
    gy, gyr, gy_send, gy_recv,
    gz, gz_send, gz_recv,
):
    zi = lax.axis_index("group")
    me = lax.axis_index("mem")
    xi, yi, ci = me // 16, (me // 2) % Y, me % 2

    def at_row(d):
        return (zi, ((xi + d // 2) % X) * 16 + yi * 2 + (ci + d % 2) % 2)

    def at_y(e):
        return (zi, xi * 16 + ((yi + e) % Y) * 2 + ci)

    def at_z(g):
        return ((zi + g) % Z, me)

    def send(src, dst, ssem, rsem, to):
        copy = pltpu.make_async_remote_copy(
            src_ref=src, dst_ref=dst, send_sem=ssem, recv_sem=rsem, device_id=to, device_id_type=MESH
        )
        copy.start()
        sent.append(copy)

    def landed(dst, rsem):
        pltpu.make_async_remote_copy(
            src_ref=dst, dst_ref=dst, send_sem=rsem, recv_sem=rsem, device_id=at_y(1), device_id_type=MESH
        ).wait_recv()

    sent = []

    barrier = pltpu.get_barrier_semaphore()
    for d in range(1, ROW):
        pl.semaphore_signal(barrier, inc=1, device_id=at_row(d), device_id_type=MESH)
    for e in range(1, Y):
        pl.semaphore_signal(barrier, inc=1, device_id=at_y(e), device_id_type=MESH)
    for g in range(1, Z):
        pl.semaphore_signal(barrier, inc=1, device_id=at_z(g), device_id_type=MESH)
    loads = [
        pltpu.make_async_copy(src, dst, load_sem.at[i])
        for i, (src, dst) in enumerate(
            ((node_hbm, node), (wm_hbm, wm), (wi_hbm, wi), (wr_hbm, wr), (ct_hbm, ct))
        )
    ]
    for load in loads:
        load.start()
    loads[0].wait()
    coltab[0] = node[...].astype(bf16)
    pl.semaphore_wait(barrier, ROW + Y + Z - 3)

    send(coltab.at[0], coltab.at[Y - 1], y_send.at[0], y_recv.at[Y - 1], at_y(1))
    send(coltab.at[0], coltab.at[1], y_send.at[1], y_recv.at[1], at_y(-1))

    owner = meta[0:16, :]
    rd = ((owner // 16 - xi) & (X - 1)) * 2 + ((owner - ci) & 1)
    re = (owner // 2 - yi) & (Y - 1)
    pair = rd * Y + re
    hot = [onehot(iota((64, BATCH), 0) == pair[j : j + 1]) for j in range(NBRS + 1)]
    before = onehot(iota((BATCH, 2 * BATCH), 0) < iota((BATCH, 2 * BATCH), 1))
    counts = mm(jnp.concatenate(hot, axis=0), before)
    run = jnp.zeros((64, BATCH), f32)
    ranks = []
    for j in range(NBRS + 1):
        part = counts[j * 64 : (j + 1) * 64]
        prior = part[:, :BATCH] + run if j < NBRS else part[:, :BATCH]
        ranks.append(jnp.sum(hot[j].astype(f32) * prior, axis=0, keepdims=True).astype(i32))
        run = run + part[:, BATCH:]
    slot_at = iota((128, BATCH), 0)
    rank_b = ranks[NBRS]
    asked = []
    for j in range(NBRS + 1):
        position = ranks[j] if j < NBRS else rank_b + CAPN
        row = meta[16 + j : 17 + j, :].astype(f32)
        asked.append(jnp.where(slot_at == position, row, 0.0).astype(bf16))
    ask_rows = mm_nt(jnp.concatenate(hot, axis=1), jnp.concatenate(asked, axis=1))
    rd_b, re_b = rd[NBRS : NBRS + 1], re[NBRS : NBRS + 1]
    inv_b = ((0 - rd_b // 2) & (X - 1)) * 2 + (rd_b & 1)
    wanted = ((slot_at & 3) == rank_b) & ((slot_at // 16) == inv_b)
    id_rows = mm_nt(
        hot[NBRS], jnp.where(wanted, meta[16 + NBRS : 17 + NBRS, :].astype(f32) + 1.0, 0.0).astype(bf16)
    )
    for d in range(ROW):
        both = jnp.concatenate([ask_rows[d * Y : (d + 1) * Y], id_rows[d * Y : (d + 1) * Y]], axis=0)
        if d == 0:
            askrecv[0] = both
        else:
            askbuf[d] = both
            send(askbuf.at[d], askrecv.at[inv_row(d)], ask_send.at[d], ask_recv.at[inv_row(d)], at_row(d))

    ages = [(meta[42:43, :] - meta[32 + j : 33 + j, :]).astype(f32) for j in range(NBRS)]
    weights = [1.0 / (1.0 + age / age_scale) for age in ages]
    total = weights[0]
    for w in weights[1:]:
        total = total + w
    for j in range(NBRS + 1):
        position = ranks[j] if j < NBRS else rank_b + CAPN
        slotrow[j : j + 1, :] = re[j : j + 1] * BLOCK + rd[j : j + 1] * SLOT + position
    for j in range(NBRS):
        slotval[j : j + 1, :] = ages[j]
        slotval[16 + j : 17 + j, :] = weights[j] / total

    for t in range(1, ROW):
        landed(askrecv.at[t], ask_recv.at[t])
    asks = askrecv[...]
    eye = onehot(iota((SLOT, 128), 0) == iota((SLOT, 128), 1))
    ask_cols = mm_nt(eye, asks[:, 0:Y].reshape(64, 128).astype(bf16)).astype(i32)

    def serve(e):
        lanes = iota((SLOT, NODE), 1)
        hit = jnp.concatenate(
            [onehot(ask_cols[:, t * Y + e : t * Y + e + 1] == lanes) for t in range(ROW)], axis=0
        )
        rows = mm(hit, coltab[e]).astype(bf16)
        slots[e, 0:SLOT] = rows[0:SLOT]
        sendbuf[e] = rows
        for t in (4, 5, 2, 3, 6, 7, 1):
            d = inv_row(t)
            send(
                sendbuf.at[e, pl.ds(t * SLOT, SLOT)], slots.at[e, pl.ds(d * SLOT, SLOT)],
                s_send.at[e, t], s_recv.at[e, d], at_row(t),
            )

    def prepare(e):
        def one(d, carry):
            first = d * SLOT
            place = iota((SLOT, BATCH), 0) + (e * BLOCK + first)
            age = jnp.zeros((SLOT, BATCH), f32)
            weight = jnp.zeros((SLOT, BATCH), f32)
            for j in range(NBRS):
                here = place == slotrow[j : j + 1, :]
                age = jnp.where(here, slotval[j : j + 1, :], age)
                weight = jnp.where(here, slotval[16 + j : 17 + j, :], weight)
            high = weight.astype(bf16)
            rows = pl.ds(pl.multiple_of(first, SLOT), SLOT)
            a_hi[e, rows] = high
            a_lo[e, rows] = (weight - high.astype(f32)).astype(bf16)
            pick[e, rows] = onehot(place == slotrow[NBRS : NBRS + 1, :])
            age = jnp.sum(age, axis=1, keepdims=True)
            turns = age * (freq[...] * (0.5 / math.pi)) + phase[...] * (0.5 / math.pi)
            turns = turns - jnp.floor(turns + 0.5)
            square = turns * turns
            value = jnp.full((SLOT, WIDTH), COS[-1], f32)
            for c in COS[-2::-1]:
                value = value * square + c
            encos[e, rows] = value
            return carry

        lax.fori_loop(0, ROW, one, 0)

    def fold(e):
        for d in range(1, ROW):
            landed(slots.at[e, pl.ds(d * SLOT, SLOT)], s_recv.at[e, d])
        got = slots[e]
        enc = (got.astype(f32) + encos[e]).astype(bf16)
        pre = mm(enc, wm[...])
        msg = (pre * sigmoid(pre)).astype(bf16)
        part = mm_tn(a_hi[e], msg) + mm_tn(a_lo[e], msg)
        mem = mm_tn(pick[e], got)
        if e == 0:
            agg[...] = part
            hid[...] = mem
        else:
            agg[...] += part
            hid[...] += mem

    serve(0)

    landed(coltab.at[Y - 1], y_recv.at[Y - 1])
    send(coltab.at[Y - 1], coltab.at[Y - 2], y_send.at[2], y_recv.at[Y - 2], at_y(1))
    landed(coltab.at[1], y_recv.at[1])
    send(coltab.at[1], coltab.at[2], y_send.at[3], y_recv.at[2], at_y(-1))
    serve(Y - 1)
    serve(1)

    ids = asks[0, Y : 2 * Y]
    for t in range(1, ROW):
        ids = ids + asks[t, Y : 2 * Y]
    idbuf[...] = ids
    for e in range(1, Y):
        send(idbuf, idrecv.at[inv_y(e)], id_send.at[e], id_recv.at[inv_y(e)], at_y(e))
    prepare(0)
    prepare(Y - 1)

    landed(coltab.at[Y - 2], y_recv.at[Y - 2])
    send(coltab.at[Y - 2], coltab.at[Y - 3], y_send.at[4], y_recv.at[Y - 3], at_y(1))
    landed(coltab.at[2], y_recv.at[2])
    send(coltab.at[2], coltab.at[3], y_send.at[5], y_recv.at[3], at_y(-1))
    serve(Y - 2)
    serve(2)
    prepare(1)
    prepare(Y - 2)
    prepare(2)

    half = NODE // 2
    landed(coltab.at[Y - 3], y_recv.at[Y - 3])
    send(
        coltab.at[Y - 3, pl.ds(0, half)], coltab.at[4, pl.ds(0, half)], y_send.at[6], y_recv.at[4], at_y(1)
    )
    landed(coltab.at[3], y_recv.at[3])
    send(
        coltab.at[3, pl.ds(half, half)], coltab.at[4, pl.ds(half, half)], y_send.at[7], y_recv.at[0], at_y(-1)
    )
    serve(Y - 3)
    serve(3)
    prepare(Y - 3)
    prepare(3)
    landed(coltab.at[4, pl.ds(0, half)], y_recv.at[4])
    landed(coltab.at[4, pl.ds(half, half)], y_recv.at[0])
    serve(4)
    prepare(4)

    target = rd_b * 128 + re_b * 16 + rank_b
    target = jnp.concatenate([target + 4 * q for q in range(4)], axis=1)
    sel[...] = onehot(iota((ROW * 128, 4 * BATCH), 0) == target)
    place = iota((1, 256), 1)
    wanted_row = ((xi + place // 64) & (X - 1)) * 128 + ((yi + (place // 8) % Y) & (Y - 1)) * 16 + (place & 7)
    for s in range(2):
        perm[s] = onehot(iota((WIDTH, 256), 0) == wanted_row + ((ci + s) & 1) * 8)
    for f in range(Y):
        if f == 0:
            line = idbuf[0:1]
        else:
            landed(idrecv.at[f], id_recv.at[f])
            line = idrecv[f, inv_y(f) : inv_y(f) + 1]
        tsc[:, f * 128 : (f + 1) * 128] = onehot(iota((NODE, 128), 0) + 1 == line.astype(i32))

    loads[1].wait()
    for e in (0, 7, 1, 6, 2, 5, 3, 4):
        fold(e)

    for load in loads[2:]:
        load.wait()
    agg_bf = agg[...].astype(bf16)
    fact[0, 0:BATCH] = mm(agg_bf, perm[0]).astype(bf16)
    fact[1, 0:BATCH] = mm(agg_bf, perm[1]).astype(bf16)
    sibling = at_row(1)
    send(fact.at[1, pl.ds(0, BATCH)], fact.at[0, pl.ds(BATCH, BATCH)], c_send.at[0], c_recv.at[0], sibling)
    hidden = hid[...]
    hid_bf = hidden.astype(bf16)

    def cols(ref, g):
        return ref[:, g * WIDTH : (g + 1) * WIDTH]

    recur = mm(hid_bf, cols(wr, 2))
    reset = sigmoid(mm(agg_bf, cols(wi, 1)) + mm(hid_bf, cols(wr, 1)))
    candidate = jnp.tanh(mm(agg_bf, cols(wi, 2)) + reset * recur)
    update = sigmoid(mm(agg_bf, cols(wi, 0)) + mm(hid_bf, cols(wr, 0)))
    up = ct[...].astype(f32)
    d_cand = up * update * (1.0 - candidate * candidate)
    d_reset = d_cand * recur * reset * (1.0 - reset)
    gap = candidate - hidden
    d_update = up * gap * update * (1.0 - update)
    parts = [d_update, d_reset, d_cand]
    for g in range(3):
        dpre[g, 0:BATCH] = parts[g].astype(bf16)
        send(
            dpre.at[g, pl.ds(0, BATCH)], dpre.at[g, pl.ds(BATCH, BATCH)],
            c_send.at[1 + g], c_recv.at[1 + g], sibling,
        )

    change = (update * gap).astype(bf16)
    change = jnp.concatenate([change[:, q * 128 : (q + 1) * 128] for q in range(4)], axis=0)
    packed = mm(sel[...], change).astype(bf16).reshape(ROW, Y, 16, 128)
    wbs[...] = packed
    wb1[:, 0] = packed[0]
    for d in (4, 5, 2, 3, 6, 7, 1):
        send(wbs.at[d], wb1.at[:, inv_row(d)], wx_send.at[d], wx_recv.at[inv_row(d)], at_row(d))

    landed(fact.at[0, pl.ds(BATCH, BATCH)], c_recv.at[0])
    mine = []
    for g in range(3):
        landed(dpre.at[g, pl.ds(BATCH, BATCH)], c_recv.at[1 + g])
        grad = mm_tn(fact[0], dpre[g])
        mine.append(grad[0:64])
        gx[g] = grad[64:256].astype(bf16)
        for k in (2, 1, 3):
            send(
                gx.at[g, pl.ds((k - 1) * 64, 64)], gxr.at[g, (-k) % X],
                gx_send.at[g, k], gx_recv.at[g, (-k) % X], at_row(2 * k),
            )

    for t in range(1, ROW):
        landed(wb1.at[:, t], wx_recv.at[t])
    for e in (4, 3, 5, 2, 6, 1, 7):
        send(wb1.at[e], wb2.at[inv_y(e)], wy_send.at[e], wy_recv.at[inv_y(e)], at_y(e))
    wb2[0] = wb1[0]

    own = []
    for g in range(3):
        acc = mine[g]
        for k in range(1, X):
            landed(gxr.at[g, k], gx_recv.at[g, k])
            acc = acc + gxr[g, k].astype(f32)
        own.append(acc[0:8])
        left, right = acc[:, 0:256], acc[:, 256:512]
        for e in (4, 3, 5, 2, 6, 1, 7):
            rows = slice(e * 8, e * 8 + 8)
            gy[g, e] = jnp.concatenate([left[rows], right[rows]], axis=0).astype(bf16)
            send(gy.at[g, e], gyr.at[g, inv_y(e)], gy_send.at[g, e], gy_recv.at[g, inv_y(e)], at_y(e))

    for g in range(3):
        acc = jnp.concatenate([own[g][:, 0:256], own[g][:, 256:512]], axis=0)
        for e in range(1, Y):
            landed(gyr.at[g, e], gy_recv.at[g, e])
            acc = acc + gyr[g, e].astype(f32)
        gz[g, zi] = acc.astype(bf16)
        for k in (4, 3, 5, 2, 6, 1, 7):
            send(gz.at[g, zi], gz.at[g, zi], gz_send.at[g, k], gz_recv.at[g, (-k) % Z], at_z(k))

    for f in range(1, Y):
        landed(wb2.at[f], wy_recv.at[f])
    back = wb2[...].reshape(Y * 128, 128)
    quarter = (iota((Y * 128, 128), 0) // 4) & 3
    wide = jnp.concatenate(
        [jnp.where(quarter == q, back.astype(f32), 0.0).astype(bf16) for q in range(4)], axis=1
    )
    out_mem[...] = node[...] + mm(tsc[...], wide)

    for g in range(3):
        for k in range(1, Z):
            landed(gz.at[g, (zi + k) % Z], gz_recv.at[g, k])
        acc = gz[g, 0].astype(f32)
        for k in range(1, Z):
            acc = acc + gz[g, k].astype(f32)
        out_grad[:, g * WIDTH : g * WIDTH + 256] = acc[0:8]
        out_grad[:, g * WIDTH + 256 : (g + 1) * WIDTH] = acc[8:16]

    for copy in sent:
        copy.wait_send()


def body(
    node_memory, batch_owner, batch_row, batch_time, neighbour_owner, neighbour_row, neighbour_time,
    frequency, phase_shift, w_message, w_input, w_recur, cotangent,
):
    near = jnp.stack(
        [neighbour_owner[0, :, 0], neighbour_row[0], neighbour_time[0]]
    ).reshape(3, BATCH, NBRS).transpose(0, 2, 1)
    core = jnp.stack([batch_owner[0, :, 0], batch_row[0], batch_time[0]]).reshape(3, 1, BATCH)
    meta = jnp.concatenate([near, core, jnp.zeros((3, 5, BATCH), i32)], axis=1).reshape(48, BATCH)
    dma = pltpu.SemaphoreType.DMA
    vmem = pl.BlockSpec(memory_space=pltpu.VMEM)
    hbm = pl.BlockSpec(memory_space=pl.ANY)
    updated, grad = pl.pallas_call(
        kernel,
        out_shape=(
            jax.ShapeDtypeStruct((NODE, WIDTH), f32),
            jax.ShapeDtypeStruct((8, 3 * WIDTH), f32),
        ),
        in_specs=[vmem] * 3 + [hbm] * 5,
        out_specs=(vmem, vmem),
        scratch_shapes=[
            pltpu.VMEM((NODE, WIDTH), f32),
            pltpu.VMEM((WIDTH, WIDTH), bf16),
            pltpu.VMEM((WIDTH, 3 * WIDTH), bf16),
            pltpu.VMEM((WIDTH, 3 * WIDTH), bf16),
            pltpu.VMEM((BATCH, WIDTH), bf16),
            dma((5,)),
            pltpu.VMEM((Y, NODE, WIDTH), bf16), dma((8,)), dma((8,)),
            pltpu.VMEM((ROW, 16, 128), f32), pltpu.VMEM((ROW, 16, 128), f32), dma((ROW,)), dma((ROW,)),
            pltpu.VMEM((Y, 128), f32), pltpu.VMEM((Y, Y, 128), f32), dma((Y,)), dma((Y,)),
            pltpu.VMEM((16, BATCH), i32),
            pltpu.VMEM((32, BATCH), f32),
            pltpu.VMEM((Y, BLOCK, WIDTH), f32),
            pltpu.VMEM((Y, BLOCK, BATCH), bf16),
            pltpu.VMEM((Y, BLOCK, BATCH), bf16),
            pltpu.VMEM((Y, BLOCK, BATCH), bf16),
            pltpu.VMEM((Y, BLOCK, WIDTH), bf16), pltpu.VMEM((Y, BLOCK, WIDTH), bf16),
            dma((Y, ROW)), dma((Y, ROW)),
            pltpu.VMEM((BATCH, WIDTH), f32), pltpu.VMEM((BATCH, WIDTH), f32),
            pltpu.VMEM((ROW * 128, 4 * BATCH), bf16),
            pltpu.VMEM((NODE, Y * 128), bf16),
            pltpu.VMEM((2, WIDTH, 256), bf16),
            pltpu.VMEM((ROW, Y, 16, 128), bf16), pltpu.VMEM((Y, ROW, 16, 128), bf16),
            pltpu.VMEM((Y, ROW, 16, 128), bf16),
            dma((ROW,)), dma((ROW,)), dma((Y,)), dma((Y,)),
            pltpu.VMEM((2, 2 * BATCH, 256), bf16), pltpu.VMEM((3, 2 * BATCH, WIDTH), bf16),
            dma((4,)), dma((4,)),
            pltpu.VMEM((3, 192, WIDTH), bf16), pltpu.VMEM((3, X, 64, WIDTH), bf16), dma((3, X)), dma((3, X)),
            pltpu.VMEM((3, Y, 16, 256), bf16), pltpu.VMEM((3, Y, 16, 256), bf16), dma((3, Y)), dma((3, Y)),
            pltpu.VMEM((3, Z, 16, 256), bf16), dma((3, Z)), dma((3, Z)),
        ],
        compiler_params=pltpu.CompilerParams(
            collective_id=0, has_side_effects=True, vmem_limit_bytes=56 * 2**20
        ),
        cost_estimate=pl.CostEstimate(flops=4 * 10**9, bytes_accessed=6 * 10**6, transcendentals=2 * 10**6),
    )(
        meta, frequency.reshape(1, WIDTH), phase_shift.reshape(1, WIDTH),
        node_memory.reshape(NODE, WIDTH), w_message, w_input, w_recur, cotangent.reshape(BATCH, WIDTH),
    )
    return updated[None], grad


def solution(mesh):
    return jax.shard_map(
        body,
        mesh=mesh,
        in_specs=(
            P("group", "mem", None),
            P("group", "mem", None),
            P("group", "mem"),
            P("group", "mem"),
            P("group", "mem", None),
            P("group", "mem"),
            P("group", "mem"),
            P(),
            P(),
            P(),
            P(),
            P(),
            P("group", "mem", None),
        ),
        out_specs=(P("group", "mem", None), P("mem", None)),
        check_vma=False,
    )
```

```python
import math

import jax
import jax.numpy as jnp
from jax import lax
from jax.experimental import pallas as pl
from jax.experimental.pallas import tpu as pltpu
from jax.sharding import PartitionSpec as P

f32, bf16, i32 = jnp.float32, jnp.bfloat16, jnp.int32
MESH = pl.DeviceIdType.MESH

age_scale = 1024.0
X, Y, Z = 4, 8, 8
ROW = 2 * X
WIDTH = 512
NODE = 256
BATCH = 128
NBRS = 10
CAPN, CAPB = 40, 4
SLOT = CAPN + CAPB
BLOCK = ROW * SLOT
STEP = 32
NEAR = (0, 1, 7, 2, 6)
COS = (
    1.0,
    -19.73920440673828,
    64.93911743164062,
    -85.45014190673828,
    60.16762924194336,
    -25.967599868774414,
    6.528658390045166,
)


def inv_row(d):
    return ((-(d // 2)) % X) * 2 + d % 2


def inv_y(e):
    return (-e) % Y


def iota(shape, dim):
    return lax.broadcasted_iota(i32, shape, dim)


def mm(a, b):
    return lax.dot_general(a, b, (((1,), (0,)), ((), ())), preferred_element_type=f32)


def mm_nt(a, b):
    return lax.dot_general(a, b, (((1,), (1,)), ((), ())), preferred_element_type=f32)


def mm_tn(a, b):
    return lax.dot_general(a, b, (((0,), (0,)), ((), ())), preferred_element_type=f32)


def onehot(mask):
    return jnp.where(mask, 1.0, 0.0).astype(bf16)


def sigmoid(v):
    return 0.5 * jnp.tanh(0.5 * v) + 0.5


def kernel(
    bo_hbm, br_hbm, bt_hbm, no_hbm, nr_hbm, nt_hbm, freq_hbm, phase_hbm,
    node_hbm, wm_hbm, wi_hbm, wr_hbm, ct_hbm,
    out_mem, out_grad,
    bo, br, bt, no, nr, nt, freq, phase, meta_sem,
    node, wm, wi, wr, ct, load_sem,
    coltab, y_send, y_recv, o_send, o_recv,
    askbuf, askrecv, ask_send, ask_recv,
    far, far_send, far_recv,
    idbuf, idone, id_send, id_recv, idsum, idtwo, idx_send, idx_recv,
    codes, encos, parts, pick,
    sendbuf, slots, s_send, s_recv,
    agg, hid, tot,
    sel, tsc, perm,
    wbs, wb1, wb2, wx_send, wx_recv, wy_send, wy_recv,
    fact, dpre, c_send, c_recv,
    gx, gxr, gx_send, gx_recv,
    gy, gyr, gy_send, gy_recv,
    gz, gz_send, gz_recv,
):
    zi = lax.axis_index("group")
    me = lax.axis_index("mem")
    xi, yi, ci = me // 16, (me // 2) % Y, me % 2

    def at_row(d):
        return (zi, ((xi + d // 2) % X) * 16 + yi * 2 + (ci + d % 2) % 2)

    def at_y(e):
        return (zi, xi * 16 + ((yi + e) % Y) * 2 + ci)

    def at_z(g):
        return ((zi + g) % Z, me)

    def send(src, dst, ssem, rsem, to):
        copy = pltpu.make_async_remote_copy(
            src_ref=src, dst_ref=dst, send_sem=ssem, recv_sem=rsem, device_id=to, device_id_type=MESH
        )
        copy.start()
        sent.append(copy)

    def landed(dst, rsem):
        pltpu.make_async_remote_copy(
            src_ref=dst, dst_ref=dst, send_sem=rsem, recv_sem=rsem, device_id=at_y(1), device_id_type=MESH
        ).wait_recv()

    sent = []

    barrier = pltpu.get_barrier_semaphore()
    for d in range(1, ROW):
        pl.semaphore_signal(barrier, inc=1, device_id=at_row(d), device_id_type=MESH)
    for e in range(1, Y):
        pl.semaphore_signal(barrier, inc=1, device_id=at_y(e), device_id_type=MESH)
    for g in range(1, Z):
        pl.semaphore_signal(barrier, inc=1, device_id=at_z(g), device_id_type=MESH)
    small = [
        pltpu.make_async_copy(src, dst, meta_sem.at[i])
        for i, (src, dst) in enumerate(
            (
                (no_hbm, no), (nr_hbm, nr), (bo_hbm, bo), (br_hbm, br),
                (nt_hbm, nt), (bt_hbm, bt), (freq_hbm, freq), (phase_hbm, phase),
            )
        )
    ]
    loads = [
        pltpu.make_async_copy(src, dst, load_sem.at[i])
        for i, (src, dst) in enumerate(
            ((node_hbm, node), (wm_hbm, wm), (wi_hbm, wi), (wr_hbm, wr), (ct_hbm, ct))
        )
    ]
    for copy in small:
        copy.start()
    loads[0].start()
    for copy in small:
        copy.wait()

    def relative(owner):
        dx = (owner // 16 - xi) & (X - 1)
        dc = (owner - ci) & 1
        return dx, dc, (owner // 2 - yi) & (Y - 1)

    dx_n, dc_n, re_n = relative(no[...])
    dx_b, dc_b, re_b = relative(bo[...])
    rd_b = dx_b * 2 + dc_b

    def lanes_of(near, core):
        return [near[:, j * BATCH : (j + 1) * BATCH] for j in range(NBRS)] + [core]

    owner_at = lanes_of((dx_n * 2 + dc_n) * Y + re_n, rd_b * Y + re_b)
    chip_at = lanes_of(dx_n * Y + re_n, dx_b * Y + re_b)
    hot = [onehot(iota((64, BATCH), 0) == o) for o in owner_at]
    before = onehot(iota((BATCH, 2 * BATCH), 0) < iota((BATCH, 2 * BATCH), 1))
    counts = mm(jnp.concatenate(hot, axis=0), before)
    run = jnp.zeros((64, BATCH), f32)
    ranks = []
    for j in range(NBRS + 1):
        part = counts[j * 64 : (j + 1) * 64]
        prior = part[:, :BATCH] + run if j < NBRS else part[:, :BATCH]
        ranks.append(jnp.sum(hot[j].astype(f32) * prior, axis=0, keepdims=True).astype(i32))
        run = run + part[:, BATCH:]
    rank_b = ranks[NBRS]
    core_at = lanes_of(dc_n, dc_b)
    position = [
        core_at[j] * SLOT + ranks[j] + (CAPN if j == NBRS else 0) for j in range(NBRS + 1)
    ]
    chips = jnp.concatenate([onehot(iota((X * Y, BATCH), 0) == o) for o in chip_at], axis=1)
    row_at = lanes_of(nr[...], br[...])
    near_at = iota((2 * SLOT, BATCH), 0)
    slot_at = iota((128, BATCH), 0)

    def placed(j, value):
        return jnp.where(slot_at == position[j], value.astype(f32), 0.0).astype(bf16)

    ask_rows = mm_nt(chips, jnp.concatenate([placed(j, row_at[j]) for j in range(NBRS + 1)], axis=1))
    for k in range(X):
        tile = ask_rows[k * Y : (k + 1) * Y]
        if k == 0:
            askrecv[0] = tile
        else:
            askbuf[k] = tile
    loads[0].wait()
    coltab[0, 0] = node[...].astype(bf16)
    pl.semaphore_wait(barrier, ROW + Y + Z - 3)

    sibling = at_row(1)
    half = NODE // 2

    def ring(e, to, step, h):
        rows = pl.ds(h * half, half)
        send(coltab.at[e, 0, rows], coltab.at[to, 0, rows], y_send.at[to, h], y_recv.at[to, h], at_y(step))

    def arrived(e, h):
        landed(coltab.at[e, 0, pl.ds(h * half, half)], y_recv.at[e, h])

    for k in (2, 1, 3):
        send(askbuf.at[k], askrecv.at[(-k) % X], ask_send.at[k], ask_recv.at[(-k) % X], at_row(2 * k))
    send(coltab.at[0, 0], coltab.at[0, 1], o_send.at[0], o_recv.at[0], sibling)
    for h in range(2):
        ring(0, Y - 1, 1, h)
        ring(0, 1, -1, h)
    send(coltab.at[0, 0], far.at[0], far_send.at[0], far_recv.at[0], at_row(4))

    wanted = ((slot_at & 3) == rank_b) & ((slot_at // 16) == ((0 - re_b) & (Y - 1)))
    id_rows = mm_nt(
        onehot(iota((64, BATCH), 0) == re_b * ROW + rd_b),
        jnp.where(wanted, br[...].astype(f32) + 1.0, 0.0).astype(bf16),
    )
    for e in range(Y):
        tile = jnp.concatenate([id_rows[e * ROW : (e + 1) * ROW], ask_rows[2 * Y : 3 * Y]], axis=0)
        if e == 0:
            idone[0] = tile
        else:
            idbuf[e] = tile
            send(idbuf.at[e], idone.at[inv_y(e)], id_send.at[e], id_recv.at[inv_y(e)], at_y(e))

    for k in range(1, X):
        landed(askrecv.at[k], ask_recv.at[k])
    asks = askrecv[...]
    eye = onehot(iota((2 * SLOT, 128), 0) == iota((2 * SLOT, 128), 1))
    ask_cols = mm_nt(eye, asks.reshape(X * Y, 128).astype(bf16)).astype(i32)
    ask_cols = ask_cols + jnp.where(iota((2 * SLOT, X * Y), 0) >= SLOT, NODE, 0)

    def hand_on(e):
        send(coltab.at[e, 0], coltab.at[e, 1], o_send.at[e], o_recv.at[e], sibling)

    def serve(e):
        landed(coltab.at[e, 1], o_recv.at[e])
        lanes = iota((2 * SLOT, 2 * NODE), 1)
        both = coltab[e].reshape(2 * NODE, WIDTH)
        for k in (2, 1, 3, 0):
            if k == 2 and e in NEAR:
                continue
            hit = onehot(ask_cols[:, k * Y + e : k * Y + e + 1] == lanes)
            rows = mm(hit, both)
            rows = jnp.concatenate([rows[:, :256], rows[:, 256:]], axis=0).astype(bf16)
            if k == 0:
                slots[e, 0] = rows
            else:
                sendbuf[e, k] = rows
                send(
                    sendbuf.at[e, k], slots.at[e, (-k) % X],
                    s_send.at[e, k], s_recv.at[e, (-k) % X], at_row(2 * k),
                )

    def serve_far():
        landed(far.at[1], far_recv.at[1])
        far_asks = jnp.concatenate([idone[f, ROW : 2 * ROW] for f in NEAR], axis=0).astype(bf16)
        far_cols = mm_nt(eye, far_asks).astype(i32)
        far_cols = far_cols + jnp.where(iota(far_cols.shape, 0) >= SLOT, NODE, 0)
        lanes = iota((2 * SLOT, 2 * NODE), 1)
        both = far[...].reshape(2 * NODE, WIDTH)
        for i, f in enumerate(NEAR):
            column = 8 * i + inv_y(f)
            rows = mm(onehot(far_cols[:, column : column + 1] == lanes), both)
            rows = jnp.concatenate([rows[:, :256], rows[:, 256:]], axis=0).astype(bf16)
            if f == 0:
                slots[0, 2] = rows
            else:
                sendbuf[f, 2] = rows
                send(
                    sendbuf.at[f, 2], slots.at[inv_y(f), 2],
                    s_send.at[f, 2], s_recv.at[inv_y(f), 2], at_y(f),
                )

    def prepare(e):
        def one(i, carry):
            rows = pl.ds(pl.multiple_of(i * STEP, STEP), STEP)
            code = codes[e, rows].astype(i32)
            here = (code >> 12) == iota((STEP, BATCH), 1) + 1
            age = jnp.where(here, (bt[...] - (code & 4095)).astype(f32), 0.0)
            weight = jnp.where(here, 1.0 / (1.0 + age / age_scale), 0.0)
            high = weight.astype(bf16)
            low = (weight - high.astype(f32)).astype(bf16)
            parts[e, rows] = jnp.concatenate([high, low], axis=1)
            pick[e, rows] = onehot(iota((STEP, BATCH), 0) + (e * BLOCK + i * STEP) == slot_b)
            age = jnp.sum(age, axis=1, keepdims=True)
            turns = age * (freq[...] * (0.5 / math.pi)) + phase[...] * (0.5 / math.pi)
            turns = turns - jnp.floor(turns + 0.5)
            square = turns * turns
            value = jnp.full((STEP, WIDTH), COS[-1], f32)
            for c in COS[-2::-1]:
                value = value * square + c
            encos[e, rows] = value
            return carry

        lax.fori_loop(0, BLOCK // STEP, one, 0, unroll=True)
        ones = jnp.ones((BLOCK, 128), bf16)
        part = mm_tn(parts[e], ones)
        part = part[:BATCH] + part[BATCH:]
        if e == 0:
            tot[...] = part
        else:
            tot[...] += part

    def fold(e):
        for k in range(1, X):
            if e or k != 2:
                landed(slots.at[e, k], s_recv.at[e, k])
        got = [slots[e, k].astype(f32) for k in range(X)]
        got = jnp.concatenate(
            [jnp.concatenate([g[: 2 * SLOT], g[2 * SLOT :]], axis=1) for g in got], axis=0
        )
        enc = (got + encos[e]).astype(bf16)
        pre = mm(enc, wm[...])
        msg = (pre * sigmoid(pre)).astype(bf16)
        part = mm_tn(parts[e], msg)
        part = part[:BATCH] + part[BATCH:]
        mem = mm_tn(pick[e], got.astype(bf16))
        if e == 0:
            agg[...] = part
            hid[...] = mem
        else:
            agg[...] += part
            hid[...] += mem

    serve(0)
    for load in loads[1:]:
        load.start()

    number = (iota((1, NBRS * BATCH), 1) * 6554) >> 16
    times = nt[...]
    values = [
        jnp.concatenate(
            [
                jnp.where(
                    near_at == position[j], value[:, j * BATCH : (j + 1) * BATCH].astype(f32), 0.0
                ).astype(bf16)
                for j in range(NBRS)
            ],
            axis=1,
        )
        for value in (number + 1, times >> 6, times & 63)
    ]
    near_chips = chips[:, : NBRS * BATCH]
    table = mm_nt(values[0], near_chips) * 4096.0
    table = table + mm_nt(values[1], near_chips) * 64.0 + mm_nt(values[2], near_chips)
    for e in range(Y):
        for k in range(X):
            column = table[:, k * Y + e : k * Y + e + 1]
            codes[e, k * 2 * SLOT : (k + 1) * 2 * SLOT] = jnp.broadcast_to(column, (2 * SLOT, BATCH))
    slot_b = re_b * BLOCK + dx_b * (2 * SLOT) + position[NBRS]


    def pass_on(e, h):
        for e, step in ((Y - e, 1), (e, -1)):
            arrived(e, h)
            if e not in (3, Y - 3) or (e == Y - 3) == (h == 0):
                ring(e, (e - step) % Y, step, h)

    prepare(0)
    pass_on(1, 0)
    pass_on(1, 1)
    hand_on(Y - 1)
    hand_on(1)
    serve(Y - 1)
    serve(1)
    prepare(Y - 1)
    pass_on(2, 0)
    prepare(1)
    pass_on(2, 1)
    hand_on(Y - 2)
    hand_on(2)
    serve(Y - 2)
    serve(2)
    landed(far.at[0], far_recv.at[0])
    send(far.at[0], far.at[1], far_send.at[1], far_recv.at[1], sibling)

    for e in range(1, Y):
        landed(idone.at[e], id_recv.at[e])
    ids = idone[0, 0:ROW]
    for e in range(1, Y):
        ids = ids + idone[e, 0:ROW]
    idsum[...] = ids
    for d in range(1, ROW):
        send(idsum, idtwo.at[inv_row(d)], idx_send.at[d], idx_recv.at[inv_row(d)], at_row(d))

    pass_on(3, 0)
    prepare(Y - 2)
    pass_on(3, 1)
    hand_on(Y - 3)
    hand_on(3)
    serve(Y - 3)
    serve(3)
    prepare(2)
    prepare(Y - 3)
    arrived(4, 0)
    arrived(4, 1)
    hand_on(4)
    serve_far()
    serve(4)

    prepare(3)
    prepare(4)
    loads[1].wait()
    for e in (0, Y - 1, 1, Y - 2, 2):
        fold(e)

    target = re_b * 128 + rd_b * 16 + rank_b
    target = jnp.concatenate([target + 4 * q for q in range(4)], axis=1)
    sel[...] = onehot(iota((Y * 128, 4 * BATCH), 0) == target)
    place = iota((1, 256), 1)
    wanted_row = ((xi + place // 64) & (X - 1)) * 128 + ((yi + (place // 8) % Y) & (Y - 1)) * 16 + (place & 7)
    for s in range(2):
        perm[s] = onehot(iota((WIDTH, 256), 0) == wanted_row + ((ci + s) & 1) * 8)
    for e in (Y - 3, 3, 4):
        fold(e)

    for load in loads[2:]:
        load.wait()
    scale = 1.0 / tot[...]
    agg_bf = (agg[...] * jnp.concatenate([scale] * 4, axis=1)).astype(bf16)
    fact[1, 0:BATCH] = mm(agg_bf, perm[1]).astype(bf16)
    send(fact.at[1, pl.ds(0, BATCH)], fact.at[0, pl.ds(BATCH, BATCH)], c_send.at[0], c_recv.at[0], sibling)
    fact[0, 0:BATCH] = mm(agg_bf, perm[0]).astype(bf16)
    hidden = hid[...]
    hid_bf = hidden.astype(bf16)

    def cols(ref, g):
        return ref[:, g * WIDTH : (g + 1) * WIDTH]

    recur = mm(hid_bf, cols(wr, 2))
    reset = sigmoid(mm(agg_bf, cols(wi, 1)) + mm(hid_bf, cols(wr, 1)))
    candidate = jnp.tanh(mm(agg_bf, cols(wi, 2)) + reset * recur)
    update = sigmoid(mm(agg_bf, cols(wi, 0)) + mm(hid_bf, cols(wr, 0)))
    up = ct[...].astype(f32)
    d_cand = up * update * (1.0 - candidate * candidate)
    d_reset = d_cand * recur * reset * (1.0 - reset)
    gap = candidate - hidden
    d_update = up * gap * update * (1.0 - update)
    for g, part in enumerate((d_update, d_reset, d_cand)):
        dpre[g, 0:BATCH] = part.astype(bf16)
        send(
            dpre.at[g, pl.ds(0, BATCH)], dpre.at[g, pl.ds(BATCH, BATCH)],
            c_send.at[1 + g], c_recv.at[1 + g], sibling,
        )

    change = (update * gap).astype(bf16)
    change = jnp.concatenate([change[:, q * 128 : (q + 1) * 128] for q in range(4)], axis=0)
    packed = mm(sel[...], change).astype(bf16).reshape(Y, ROW, 16, 128)
    wbs[...] = packed
    wb1[:, 0] = packed[0]
    for e in (4, 3, 5, 2, 6, 1, 7):
        send(wbs.at[e], wb1.at[:, inv_y(e)], wy_send.at[e], wy_recv.at[inv_y(e)], at_y(e))

    landed(fact.at[0, pl.ds(BATCH, BATCH)], c_recv.at[0])
    mine = []
    for g in range(3):
        landed(dpre.at[g, pl.ds(BATCH, BATCH)], c_recv.at[1 + g])
        grad = mm_tn(fact[0], dpre[g])
        mine.append(grad[0:64])
        gx[g] = grad[64:256].astype(bf16)
        for k in (2, 1, 3):
            send(
                gx.at[g, pl.ds((k - 1) * 64, 64)], gxr.at[g, (-k) % X],
                gx_send.at[g, k], gx_recv.at[g, (-k) % X], at_row(2 * k),
            )

    for d in range(ROW):
        if d == 0:
            line = idsum[0:1]
        else:
            landed(idtwo.at[d], idx_recv.at[d])
            line = idtwo[d, inv_row(d) : inv_row(d) + 1]
        tsc[:, d * 128 : (d + 1) * 128] = onehot(iota((NODE, 128), 0) + 1 == line.astype(i32))

    own = []
    for g in range(3):
        acc = mine[g]
        for k in range(1, X):
            landed(gxr.at[g, k], gx_recv.at[g, k])
            acc = acc + gxr[g, k].astype(f32)
        own.append(acc[0:8])
        left, right = acc[:, 0:256], acc[:, 256:512]
        for e in (4, 3, 5, 2, 6, 1, 7):
            rows = slice(e * 8, e * 8 + 8)
            gy[g, e] = jnp.concatenate([left[rows], right[rows]], axis=0).astype(bf16)
            send(gy.at[g, e], gyr.at[g, inv_y(e)], gy_send.at[g, e], gy_recv.at[g, inv_y(e)], at_y(e))

    for e in range(1, Y):
        landed(wb1.at[:, e], wy_recv.at[e])
    for d in (4, 5, 2, 3, 6, 7, 1):
        send(wb1.at[d], wb2.at[inv_row(d)], wx_send.at[d], wx_recv.at[inv_row(d)], at_row(d))
    wb2[0] = wb1[0]

    for g in range(3):
        acc = jnp.concatenate([own[g][:, 0:256], own[g][:, 256:512]], axis=0)
        for e in range(1, Y):
            landed(gyr.at[g, e], gy_recv.at[g, e])
            acc = acc + gyr[g, e].astype(f32)
        gz[g, zi] = acc.astype(bf16)
        for k in (4, 3, 5, 2, 6, 1, 7):
            send(gz.at[g, zi], gz.at[g, zi], gz_send.at[g, k], gz_recv.at[g, (-k) % Z], at_z(k))

    for d in range(1, ROW):
        landed(wb2.at[d], wx_recv.at[d])
    back = wb2[...].reshape(ROW * 128, 128)
    quarter = (iota((ROW * 128, 128), 0) // 4) & 3
    wide = jnp.concatenate(
        [jnp.where(quarter == q, back.astype(f32), 0.0).astype(bf16) for q in range(4)], axis=1
    )
    out_mem[...] = mm(tsc[...], wide)

    for g in range(3):
        for k in range(1, Z):
            landed(gz.at[g, (zi + k) % Z], gz_recv.at[g, k])
        for h in range(2):
            acc = gz[g, 4 * h].astype(f32)
            for k in range(1, 4):
                acc = acc + gz[g, 4 * h + k].astype(f32)
            out_grad[h, :, g * WIDTH : g * WIDTH + 256] = acc[0:8]
            out_grad[h, :, g * WIDTH + 256 : (g + 1) * WIDTH] = acc[8:16]

    for copy in sent:
        copy.wait_send()


def body(
    node_memory, batch_owner, batch_row, batch_time, neighbour_owner, neighbour_row, neighbour_time,
    frequency, phase_shift, w_message, w_input, w_recur, cotangent,
):
    dma = pltpu.SemaphoreType.DMA
    vmem = pl.BlockSpec(memory_space=pltpu.VMEM)
    hbm = pl.BlockSpec(memory_space=pl.ANY)
    rows = NBRS * BATCH
    owned = node_memory.reshape(NODE, WIDTH)
    change, grad = pl.pallas_call(
        kernel,
        out_shape=(
            jax.ShapeDtypeStruct((NODE, WIDTH), f32),
            jax.ShapeDtypeStruct((2, 8, 3 * WIDTH), f32),
        ),
        in_specs=[hbm] * 13,
        out_specs=(vmem, vmem),
        scratch_shapes=[
            pltpu.VMEM((1, BATCH), i32), pltpu.VMEM((1, BATCH), i32), pltpu.VMEM((1, BATCH), i32),
            pltpu.VMEM((1, rows), i32), pltpu.VMEM((1, rows), i32), pltpu.VMEM((1, rows), i32),
            pltpu.VMEM((1, WIDTH), f32), pltpu.VMEM((1, WIDTH), f32),
            dma((8,)),
            pltpu.VMEM((NODE, WIDTH), f32),
            pltpu.VMEM((WIDTH, WIDTH), bf16),
            pltpu.VMEM((WIDTH, 3 * WIDTH), bf16),
            pltpu.VMEM((WIDTH, 3 * WIDTH), bf16),
            pltpu.VMEM((BATCH, WIDTH), bf16),
            dma((5,)),
            pltpu.VMEM((Y, 2, NODE, WIDTH), bf16), dma((Y, 2)), dma((Y, 2)), dma((Y,)), dma((Y,)),
            pltpu.VMEM((X, Y, 128), f32), pltpu.VMEM((X, Y, 128), f32), dma((X,)), dma((X,)),
            pltpu.VMEM((2, NODE, WIDTH), bf16), dma((2,)), dma((2,)),
            pltpu.VMEM((Y, 2 * ROW, 128), f32), pltpu.VMEM((Y, 2 * ROW, 128), f32), dma((Y,)), dma((Y,)),
            pltpu.VMEM((ROW, 128), f32), pltpu.VMEM((ROW, ROW, 128), f32), dma((ROW,)), dma((ROW,)),
            pltpu.VMEM((Y, BLOCK, BATCH), f32),
            pltpu.VMEM((Y, BLOCK, WIDTH), f32),
            pltpu.VMEM((Y, BLOCK, 2 * BATCH), bf16),
            pltpu.VMEM((Y, BLOCK, BATCH), bf16),
            pltpu.VMEM((Y, X, 4 * SLOT, 256), bf16), pltpu.VMEM((Y, X, 4 * SLOT, 256), bf16),
            dma((Y, X)), dma((Y, X)),
            pltpu.VMEM((BATCH, WIDTH), f32), pltpu.VMEM((BATCH, WIDTH), f32), pltpu.VMEM((BATCH, 128), f32),
            pltpu.VMEM((Y * 128, 4 * BATCH), bf16),
            pltpu.VMEM((NODE, ROW * 128), bf16),
            pltpu.VMEM((2, WIDTH, 256), bf16),
            pltpu.VMEM((Y, ROW, 16, 128), bf16), pltpu.VMEM((ROW, Y, 16, 128), bf16),
            pltpu.VMEM((ROW, Y, 16, 128), bf16),
            dma((ROW,)), dma((ROW,)), dma((Y,)), dma((Y,)),
            pltpu.VMEM((2, 2 * BATCH, 256), bf16), pltpu.VMEM((3, 2 * BATCH, WIDTH), bf16),
            dma((4,)), dma((4,)),
            pltpu.VMEM((3, 192, WIDTH), bf16), pltpu.VMEM((3, X, 64, WIDTH), bf16), dma((3, X)), dma((3, X)),
            pltpu.VMEM((3, Y, 16, 256), bf16), pltpu.VMEM((3, Y, 16, 256), bf16), dma((3, Y)), dma((3, Y)),
            pltpu.VMEM((3, Z, 16, 256), bf16), dma((3, Z)), dma((3, Z)),
        ],
        compiler_params=pltpu.CompilerParams(
            collective_id=0, has_side_effects=True, vmem_limit_bytes=60 * 2**20
        ),
        cost_estimate=pl.CostEstimate(flops=4 * 10**9, bytes_accessed=6 * 10**6, transcendentals=2 * 10**6),
    )(
        batch_owner.reshape(1, BATCH), batch_row, batch_time,
        neighbour_owner.reshape(1, rows), neighbour_row, neighbour_time,
        frequency.reshape(1, WIDTH), phase_shift.reshape(1, WIDTH),
        owned, w_message, w_input, w_recur, cotangent.reshape(BATCH, WIDTH),
    )
    return (owned + change)[None], grad[0] + grad[1]


def solution(mesh):
    return jax.shard_map(
        body,
        mesh=mesh,
        in_specs=(
            P("group", "mem", None),
            P("group", "mem", None),
            P("group", "mem"),
            P("group", "mem"),
            P("group", "mem", None),
            P("group", "mem"),
            P("group", "mem"),
            P(),
            P(),
            P(),
            P(),
            P(),
            P("group", "mem", None),
        ),
        out_specs=(P("group", "mem", None), P("mem", None)),
        check_vma=False,
    )
```

```python
import math

import jax
import jax.numpy as jnp
from jax import lax
from jax.experimental import pallas as pl
from jax.experimental.pallas import tpu as pltpu
from jax.sharding import PartitionSpec as P

f32, bf16, i32 = jnp.float32, jnp.bfloat16, jnp.int32
MESH = pl.DeviceIdType.MESH

age_scale = 1024.0
X, Y, Z = 4, 8, 8
ROW = 2 * X
WIDTH = 512
NODE = 256
BATCH = 128
NBRS = 10
CAPN, CAPB = 40, 4
SLOT = CAPN + CAPB
BLOCK = ROW * SLOT
STEP = 32
NEAR = (0, 1, 7, 2, 6)
COS = (
    1.0,
    -19.73920440673828,
    64.93911743164062,
    -85.45014190673828,
    60.16762924194336,
    -25.967599868774414,
    6.528658390045166,
)


def inv_row(d):
    return ((-(d // 2)) % X) * 2 + d % 2


def inv_y(e):
    return (-e) % Y


def iota(shape, dim):
    return lax.broadcasted_iota(i32, shape, dim)


def mm(a, b):
    return lax.dot_general(a, b, (((1,), (0,)), ((), ())), preferred_element_type=f32)


def mm_nt(a, b):
    return lax.dot_general(a, b, (((1,), (1,)), ((), ())), preferred_element_type=f32)


def mm_tn(a, b):
    return lax.dot_general(a, b, (((0,), (0,)), ((), ())), preferred_element_type=f32)


def onehot(mask):
    return jnp.where(mask, 1.0, 0.0).astype(bf16)


def sigmoid(v):
    return 0.5 * jnp.tanh(0.5 * v) + 0.5


def kernel(
    bo_hbm, br_hbm, bt_hbm, no_hbm, nr_hbm, nt_hbm, freq_hbm, phase_hbm,
    node_hbm, wm_hbm, wi_hbm, wr_hbm, ct_hbm,
    out_mem, out_grad,
    bo, br, bt, no, nr, nt, freq, phase, meta_sem,
    node, wm, wi, wr, ct, load_sem,
    coltab, y_send, y_recv, o_send, o_recv,
    askbuf, askrecv, ask_send, ask_recv,
    far, far_send, far_recv,
    idbuf, idone, id_send, id_recv, idsum, idtwo, idx_send, idx_recv,
    codes, encos, parts, pick,
    sendbuf, slots, s_send, s_recv,
    agg, hid, tot,
    sel, tsc, perm,
    wbs, wb1, wb2, wx_send, wx_recv, wy_send, wy_recv,
    fact, dpre, c_send, c_recv,
    gx, gxr, gx_send, gx_recv,
    gy, gyr, gy_send, gy_recv,
    gz, gz_send, gz_recv,
):
    zi = lax.axis_index("group")
    me = lax.axis_index("mem")
    xi, yi, ci = me // 16, (me // 2) % Y, me % 2

    def at_row(d):
        return (zi, ((xi + d // 2) % X) * 16 + yi * 2 + (ci + d % 2) % 2)

    def at_y(e):
        return (zi, xi * 16 + ((yi + e) % Y) * 2 + ci)

    def at_z(g):
        return ((zi + g) % Z, me)

    def send(src, dst, ssem, rsem, to):
        copy = pltpu.make_async_remote_copy(
            src_ref=src, dst_ref=dst, send_sem=ssem, recv_sem=rsem, device_id=to, device_id_type=MESH
        )
        copy.start()
        sent.append(copy)

    def landed(dst, rsem):
        pltpu.make_async_remote_copy(
            src_ref=dst, dst_ref=dst, send_sem=rsem, recv_sem=rsem, device_id=at_y(1), device_id_type=MESH
        ).wait_recv()

    sent = []

    barrier = pltpu.get_barrier_semaphore()
    for d in range(1, ROW):
        pl.semaphore_signal(barrier, inc=1, device_id=at_row(d), device_id_type=MESH)
    for e in range(1, Y):
        pl.semaphore_signal(barrier, inc=1, device_id=at_y(e), device_id_type=MESH)
    for g in range(1, Z):
        pl.semaphore_signal(barrier, inc=1, device_id=at_z(g), device_id_type=MESH)
    small = [
        pltpu.make_async_copy(src, dst, meta_sem.at[i])
        for i, (src, dst) in enumerate(
            (
                (no_hbm, no), (nr_hbm, nr), (bo_hbm, bo), (br_hbm, br),
                (nt_hbm, nt), (bt_hbm, bt), (freq_hbm, freq), (phase_hbm, phase),
            )
        )
    ]
    loads = [
        pltpu.make_async_copy(src, dst, load_sem.at[i])
        for i, (src, dst) in enumerate(
            ((node_hbm, node), (wm_hbm, wm), (wi_hbm, wi), (wr_hbm, wr), (ct_hbm, ct))
        )
    ]
    for copy in small:
        copy.start()
    loads[0].start()
    for copy in small:
        copy.wait()

    def relative(owner):
        dx = (owner // 16 - xi) & (X - 1)
        dc = (owner - ci) & 1
        return dx, dc, (owner // 2 - yi) & (Y - 1)

    dx_n, dc_n, re_n = relative(no[...])
    dx_b, dc_b, re_b = relative(bo[...])
    rd_b = dx_b * 2 + dc_b

    def lanes_of(near, core):
        return [near[:, j * BATCH : (j + 1) * BATCH] for j in range(NBRS)] + [core]

    owner_at = lanes_of((dx_n * 2 + dc_n) * Y + re_n, rd_b * Y + re_b)
    chip_at = lanes_of(dx_n * Y + re_n, dx_b * Y + re_b)
    hot = [onehot(iota((64, BATCH), 0) == o) for o in owner_at]
    before = onehot(iota((BATCH, 2 * BATCH), 0) < iota((BATCH, 2 * BATCH), 1))
    counts = mm(jnp.concatenate(hot, axis=0), before)
    run = jnp.zeros((64, BATCH), f32)
    ranks = []
    for j in range(NBRS + 1):
        part = counts[j * 64 : (j + 1) * 64]
        prior = part[:, :BATCH] + run if j < NBRS else part[:, :BATCH]
        ranks.append(jnp.sum(hot[j].astype(f32) * prior, axis=0, keepdims=True).astype(i32))
        run = run + part[:, BATCH:]
    rank_b = ranks[NBRS]
    core_at = lanes_of(dc_n, dc_b)
    position = [
        core_at[j] * SLOT + ranks[j] + (CAPN if j == NBRS else 0) for j in range(NBRS + 1)
    ]
    chips = jnp.concatenate([onehot(iota((X * Y, BATCH), 0) == o) for o in chip_at], axis=1)
    row_at = lanes_of(nr[...], br[...])
    near_at = iota((2 * SLOT, BATCH), 0)
    slot_at = iota((128, BATCH), 0)

    def placed(j, value):
        return jnp.where(slot_at == position[j], value.astype(f32), 0.0).astype(bf16)

    ask_rows = mm_nt(chips, jnp.concatenate([placed(j, row_at[j]) for j in range(NBRS + 1)], axis=1))
    for k in range(X):
        tile = ask_rows[k * Y : (k + 1) * Y]
        if k == 0:
            askrecv[0] = tile
        else:
            askbuf[k] = tile
    loads[0].wait()
    coltab[0, 0] = node[...].astype(bf16)
    pl.semaphore_wait(barrier, ROW + Y + Z - 3)

    sibling = at_row(1)
    half = NODE // 2

    def ring(e, to, step, h):
        rows = pl.ds(h * half, half)
        send(coltab.at[e, 0, rows], coltab.at[to, 0, rows], y_send.at[to, h], y_recv.at[to, h], at_y(step))

    def arrived(e, h):
        landed(coltab.at[e, 0, pl.ds(h * half, half)], y_recv.at[e, h])

    for k in (2, 1, 3):
        send(askbuf.at[k], askrecv.at[(-k) % X], ask_send.at[k], ask_recv.at[(-k) % X], at_row(2 * k))
    send(coltab.at[0, 0], coltab.at[0, 1], o_send.at[0], o_recv.at[0], sibling)
    for h in range(2):
        ring(0, Y - 1, 1, h)
        ring(0, 1, -1, h)
    send(coltab.at[0, 0], far.at[0], far_send.at[0], far_recv.at[0], at_row(4))

    wanted = ((slot_at & 3) == rank_b) & ((slot_at // 16) == ((0 - re_b) & (Y - 1)))
    id_rows = mm_nt(
        onehot(iota((64, BATCH), 0) == re_b * ROW + rd_b),
        jnp.where(wanted, br[...].astype(f32) + 1.0, 0.0).astype(bf16),
    )
    for e in range(Y):
        tile = jnp.concatenate([id_rows[e * ROW : (e + 1) * ROW], ask_rows[2 * Y : 3 * Y]], axis=0)
        if e == 0:
            idone[0] = tile
        else:
            idbuf[e] = tile
            send(idbuf.at[e], idone.at[inv_y(e)], id_send.at[e], id_recv.at[inv_y(e)], at_y(e))

    for k in range(1, X):
        landed(askrecv.at[k], ask_recv.at[k])
    asks = askrecv[...]
    eye = onehot(iota((2 * SLOT, 128), 0) == iota((2 * SLOT, 128), 1))
    ask_cols = mm_nt(eye, asks.reshape(X * Y, 128).astype(bf16)).astype(i32)
    ask_cols = ask_cols + jnp.where(iota((2 * SLOT, X * Y), 0) >= SLOT, NODE, 0)

    def hand_on(e):
        send(coltab.at[e, 0], coltab.at[e, 1], o_send.at[e], o_recv.at[e], sibling)

    def serve(e):
        landed(coltab.at[e, 1], o_recv.at[e])
        lanes = iota((2 * SLOT, 2 * NODE), 1)
        both = coltab[e].reshape(2 * NODE, WIDTH)
        for k in (2, 1, 3, 0):
            if k == 2 and e in NEAR:
                continue
            hit = onehot(ask_cols[:, k * Y + e : k * Y + e + 1] == lanes)
            rows = mm(hit, both)
            rows = jnp.concatenate([rows[:, :256], rows[:, 256:]], axis=0).astype(bf16)
            if k == 0:
                slots[e, 0] = rows
            else:
                sendbuf[e, k] = rows
                send(
                    sendbuf.at[e, k], slots.at[e, (-k) % X],
                    s_send.at[e, k], s_recv.at[e, (-k) % X], at_row(2 * k),
                )

    def serve_far():
        landed(far.at[1], far_recv.at[1])
        far_asks = jnp.concatenate([idone[f, ROW : 2 * ROW] for f in NEAR], axis=0).astype(bf16)
        far_cols = mm_nt(eye, far_asks).astype(i32)
        far_cols = far_cols + jnp.where(iota(far_cols.shape, 0) >= SLOT, NODE, 0)
        lanes = iota((2 * SLOT, 2 * NODE), 1)
        both = far[...].reshape(2 * NODE, WIDTH)
        for i, f in enumerate(NEAR):
            column = 8 * i + inv_y(f)
            rows = mm(onehot(far_cols[:, column : column + 1] == lanes), both)
            rows = jnp.concatenate([rows[:, :256], rows[:, 256:]], axis=0).astype(bf16)
            if f == 0:
                slots[0, 2] = rows
            else:
                sendbuf[f, 2] = rows
                send(
                    sendbuf.at[f, 2], slots.at[inv_y(f), 2],
                    s_send.at[f, 2], s_recv.at[inv_y(f), 2], at_y(f),
                )

    def prepare(e):
        def one(i, carry):
            rows = pl.ds(pl.multiple_of(i * STEP, STEP), STEP)
            code = codes[e, rows].astype(i32)
            here = (code >> 12) == iota((STEP, BATCH), 1) + 1
            age = jnp.where(here, (bt[...] - (code & 4095)).astype(f32), 0.0)
            weight = jnp.where(here, 1.0 / (1.0 + age / age_scale), 0.0)
            high = weight.astype(bf16)
            low = (weight - high.astype(f32)).astype(bf16)
            parts[e, rows] = jnp.concatenate([high, low], axis=1)
            pick[e, rows] = onehot(iota((STEP, BATCH), 0) + (e * BLOCK + i * STEP) == slot_b)
            age = jnp.sum(age, axis=1, keepdims=True)
            turns = age * (freq[...] * (0.5 / math.pi)) + phase[...] * (0.5 / math.pi)
            turns = turns - jnp.floor(turns + 0.5)
            square = turns * turns
            value = jnp.full((STEP, WIDTH), COS[-1], f32)
            for c in COS[-2::-1]:
                value = value * square + c
            encos[e, rows] = value
            return carry

        lax.fori_loop(0, BLOCK // STEP, one, 0, unroll=True)
        ones = jnp.ones((BLOCK, 128), bf16)
        part = mm_tn(parts[e], ones)
        part = part[:BATCH] + part[BATCH:]
        if e == 0:
            tot[...] = part
        else:
            tot[...] += part

    def fold(e):
        for k in range(1, X):
            if e or k != 2:
                landed(slots.at[e, k], s_recv.at[e, k])
        got = [slots[e, k].astype(f32) for k in range(X)]
        got = jnp.concatenate(
            [jnp.concatenate([g[: 2 * SLOT], g[2 * SLOT :]], axis=1) for g in got], axis=0
        )
        enc = (got + encos[e]).astype(bf16)
        pre = mm(enc, wm[...])
        msg = (pre * sigmoid(pre)).astype(bf16)
        part = mm_tn(parts[e], msg)
        part = part[:BATCH] + part[BATCH:]
        mem = mm_tn(pick[e], got.astype(bf16))
        if e == 0:
            agg[...] = part
            hid[...] = mem
        else:
            agg[...] += part
            hid[...] += mem

    serve(0)
    for load in loads[1:]:
        load.start()

    number = (iota((1, NBRS * BATCH), 1) * 6554) >> 16
    times = nt[...]
    values = [
        jnp.concatenate(
            [
                jnp.where(
                    near_at == position[j], value[:, j * BATCH : (j + 1) * BATCH].astype(f32), 0.0
                ).astype(bf16)
                for j in range(NBRS)
            ],
            axis=1,
        )
        for value in (number + 1, times >> 6, times & 63)
    ]
    near_chips = chips[:, : NBRS * BATCH]
    table = mm_nt(values[0], near_chips) * 4096.0
    table = table + mm_nt(values[1], near_chips) * 64.0 + mm_nt(values[2], near_chips)
    for e in range(Y):
        for k in range(X):
            column = table[:, k * Y + e : k * Y + e + 1]
            codes[e, k * 2 * SLOT : (k + 1) * 2 * SLOT] = jnp.broadcast_to(column, (2 * SLOT, BATCH))
    slot_b = re_b * BLOCK + dx_b * (2 * SLOT) + position[NBRS]


    def pass_on(e, h):
        for e, step in ((Y - e, 1), (e, -1)):
            arrived(e, h)
            if e not in (3, Y - 3) or (e == Y - 3) == (h == 0):
                ring(e, (e - step) % Y, step, h)

    prepare(0)
    pass_on(1, 0)
    pass_on(1, 1)
    hand_on(Y - 1)
    hand_on(1)
    serve(Y - 1)
    serve(1)
    prepare(Y - 1)
    pass_on(2, 0)
    prepare(1)
    pass_on(2, 1)
    hand_on(Y - 2)
    hand_on(2)
    serve(Y - 2)
    serve(2)
    landed(far.at[0], far_recv.at[0])
    send(far.at[0], far.at[1], far_send.at[1], far_recv.at[1], sibling)

    for e in range(1, Y):
        landed(idone.at[e], id_recv.at[e])
    ids = idone[0, 0:ROW]
    for e in range(1, Y):
        ids = ids + idone[e, 0:ROW]
    idsum[...] = ids
    for d in range(1, ROW):
        send(idsum, idtwo.at[inv_row(d)], idx_send.at[d], idx_recv.at[inv_row(d)], at_row(d))

    pass_on(3, 0)
    prepare(Y - 2)
    pass_on(3, 1)
    hand_on(Y - 3)
    hand_on(3)
    serve(Y - 3)
    serve(3)
    serve_far()
    prepare(2)
    prepare(Y - 3)
    arrived(4, 0)
    arrived(4, 1)
    hand_on(4)
    serve(4)

    prepare(3)
    prepare(4)
    loads[1].wait()
    for e in (0, Y - 1, 1, Y - 2, 2):
        fold(e)

    target = re_b * 128 + rd_b * 16 + rank_b
    target = jnp.concatenate([target + 4 * q for q in range(4)], axis=1)
    sel[...] = onehot(iota((Y * 128, 4 * BATCH), 0) == target)
    place = iota((1, 256), 1)
    wanted_row = ((xi + place // 64) & (X - 1)) * 128 + ((yi + (place // 8) % Y) & (Y - 1)) * 16 + (place & 7)
    for s in range(2):
        perm[s] = onehot(iota((WIDTH, 256), 0) == wanted_row + ((ci + s) & 1) * 8)
    for e in (Y - 3, 3, 4):
        fold(e)

    for load in loads[2:]:
        load.wait()
    scale = 1.0 / tot[...]
    agg_bf = (agg[...] * jnp.concatenate([scale] * 4, axis=1)).astype(bf16)
    fact[1, 0:BATCH] = mm(agg_bf, perm[1]).astype(bf16)
    send(fact.at[1, pl.ds(0, BATCH)], fact.at[0, pl.ds(BATCH, BATCH)], c_send.at[0], c_recv.at[0], sibling)
    fact[0, 0:BATCH] = mm(agg_bf, perm[0]).astype(bf16)
    hidden = hid[...]
    hid_bf = hidden.astype(bf16)

    def cols(ref, g):
        return ref[:, g * WIDTH : (g + 1) * WIDTH]

    recur = mm(hid_bf, cols(wr, 2))
    reset = sigmoid(mm(agg_bf, cols(wi, 1)) + mm(hid_bf, cols(wr, 1)))
    candidate = jnp.tanh(mm(agg_bf, cols(wi, 2)) + reset * recur)
    update = sigmoid(mm(agg_bf, cols(wi, 0)) + mm(hid_bf, cols(wr, 0)))
    up = ct[...].astype(f32)
    d_cand = up * update * (1.0 - candidate * candidate)
    d_reset = d_cand * recur * reset * (1.0 - reset)
    gap = candidate - hidden
    d_update = up * gap * update * (1.0 - update)
    for g, part in enumerate((d_update, d_reset, d_cand)):
        dpre[g, 0:BATCH] = part.astype(bf16)
        send(
            dpre.at[g, pl.ds(0, BATCH)], dpre.at[g, pl.ds(BATCH, BATCH)],
            c_send.at[1 + g], c_recv.at[1 + g], sibling,
        )

    change = (update * gap).astype(bf16)
    change = jnp.concatenate([change[:, q * 128 : (q + 1) * 128] for q in range(4)], axis=0)
    packed = mm(sel[...], change).astype(bf16).reshape(Y, ROW, 16, 128)
    wbs[...] = packed
    wb1[:, 0] = packed[0]
    for e in (4, 3, 5, 2, 6, 1, 7):
        send(wbs.at[e], wb1.at[:, inv_y(e)], wy_send.at[e], wy_recv.at[inv_y(e)], at_y(e))

    landed(fact.at[0, pl.ds(BATCH, BATCH)], c_recv.at[0])
    mine = []
    for g in range(3):
        landed(dpre.at[g, pl.ds(BATCH, BATCH)], c_recv.at[1 + g])
        grad = mm_tn(fact[0], dpre[g])
        mine.append(grad[0:64])
        gx[g] = grad[64:256].astype(bf16)
        for k in (2, 1, 3):
            send(
                gx.at[g, pl.ds((k - 1) * 64, 64)], gxr.at[g, (-k) % X],
                gx_send.at[g, k], gx_recv.at[g, (-k) % X], at_row(2 * k),
            )

    for d in range(ROW):
        if d == 0:
            line = idsum[0:1]
        else:
            landed(idtwo.at[d], idx_recv.at[d])
            line = idtwo[d, inv_row(d) : inv_row(d) + 1]
        tsc[:, d * 128 : (d + 1) * 128] = onehot(iota((NODE, 128), 0) + 1 == line.astype(i32))

    own = []
    for g in range(3):
        acc = mine[g]
        for k in range(1, X):
            landed(gxr.at[g, k], gx_recv.at[g, k])
            acc = acc + gxr[g, k].astype(f32)
        own.append(acc[0:8])
        left, right = acc[:, 0:256], acc[:, 256:512]
        for e in (4, 3, 5, 2, 6, 1, 7):
            rows = slice(e * 8, e * 8 + 8)
            gy[g, e] = jnp.concatenate([left[rows], right[rows]], axis=0).astype(bf16)
            send(gy.at[g, e], gyr.at[g, inv_y(e)], gy_send.at[g, e], gy_recv.at[g, inv_y(e)], at_y(e))

    for e in range(1, Y):
        landed(wb1.at[:, e], wy_recv.at[e])
    for d in (4, 5, 2, 3, 6, 7, 1):
        send(wb1.at[d], wb2.at[inv_row(d)], wx_send.at[d], wx_recv.at[inv_row(d)], at_row(d))
    wb2[0] = wb1[0]

    for g in range(3):
        acc = jnp.concatenate([own[g][:, 0:256], own[g][:, 256:512]], axis=0)
        for e in range(1, Y):
            landed(gyr.at[g, e], gy_recv.at[g, e])
            acc = acc + gyr[g, e].astype(f32)
        gz[g, zi] = acc.astype(bf16)
        for k in (4, 3, 5, 2, 6, 1, 7):
            send(gz.at[g, zi], gz.at[g, zi], gz_send.at[g, k], gz_recv.at[g, (-k) % Z], at_z(k))

    for d in range(1, ROW):
        landed(wb2.at[d], wx_recv.at[d])
    back = wb2[...].reshape(ROW * 128, 128)
    quarter = (iota((ROW * 128, 128), 0) // 4) & 3
    wide = jnp.concatenate(
        [jnp.where(quarter == q, back.astype(f32), 0.0).astype(bf16) for q in range(4)], axis=1
    )
    out_mem[...] = mm(tsc[...], wide)

    for g in range(3):
        for k in range(1, Z):
            landed(gz.at[g, (zi + k) % Z], gz_recv.at[g, k])
        for h in range(2):
            acc = gz[g, 4 * h].astype(f32)
            for k in range(1, 4):
                acc = acc + gz[g, 4 * h + k].astype(f32)
            out_grad[h, :, g * WIDTH : g * WIDTH + 256] = acc[0:8]
            out_grad[h, :, g * WIDTH + 256 : (g + 1) * WIDTH] = acc[8:16]

    for copy in sent:
        copy.wait_send()


def body(
    node_memory, batch_owner, batch_row, batch_time, neighbour_owner, neighbour_row, neighbour_time,
    frequency, phase_shift, w_message, w_input, w_recur, cotangent,
):
    dma = pltpu.SemaphoreType.DMA
    vmem = pl.BlockSpec(memory_space=pltpu.VMEM)
    hbm = pl.BlockSpec(memory_space=pl.ANY)
    rows = NBRS * BATCH
    owned = node_memory.reshape(NODE, WIDTH)
    change, grad = pl.pallas_call(
        kernel,
        out_shape=(
            jax.ShapeDtypeStruct((NODE, WIDTH), f32),
            jax.ShapeDtypeStruct((2, 8, 3 * WIDTH), f32),
        ),
        in_specs=[hbm] * 13,
        out_specs=(vmem, vmem),
        scratch_shapes=[
            pltpu.VMEM((1, BATCH), i32), pltpu.VMEM((1, BATCH), i32), pltpu.VMEM((1, BATCH), i32),
            pltpu.VMEM((1, rows), i32), pltpu.VMEM((1, rows), i32), pltpu.VMEM((1, rows), i32),
            pltpu.VMEM((1, WIDTH), f32), pltpu.VMEM((1, WIDTH), f32),
            dma((8,)),
            pltpu.VMEM((NODE, WIDTH), f32),
            pltpu.VMEM((WIDTH, WIDTH), bf16),
            pltpu.VMEM((WIDTH, 3 * WIDTH), bf16),
            pltpu.VMEM((WIDTH, 3 * WIDTH), bf16),
            pltpu.VMEM((BATCH, WIDTH), bf16),
            dma((5,)),
            pltpu.VMEM((Y, 2, NODE, WIDTH), bf16), dma((Y, 2)), dma((Y, 2)), dma((Y,)), dma((Y,)),
            pltpu.VMEM((X, Y, 128), f32), pltpu.VMEM((X, Y, 128), f32), dma((X,)), dma((X,)),
            pltpu.VMEM((2, NODE, WIDTH), bf16), dma((2,)), dma((2,)),
            pltpu.VMEM((Y, 2 * ROW, 128), f32), pltpu.VMEM((Y, 2 * ROW, 128), f32), dma((Y,)), dma((Y,)),
            pltpu.VMEM((ROW, 128), f32), pltpu.VMEM((ROW, ROW, 128), f32), dma((ROW,)), dma((ROW,)),
            pltpu.VMEM((Y, BLOCK, BATCH), f32),
            pltpu.VMEM((Y, BLOCK, WIDTH), f32),
            pltpu.VMEM((Y, BLOCK, 2 * BATCH), bf16),
            pltpu.VMEM((Y, BLOCK, BATCH), bf16),
            pltpu.VMEM((Y, X, 4 * SLOT, 256), bf16), pltpu.VMEM((Y, X, 4 * SLOT, 256), bf16),
            dma((Y, X)), dma((Y, X)),
            pltpu.VMEM((BATCH, WIDTH), f32), pltpu.VMEM((BATCH, WIDTH), f32), pltpu.VMEM((BATCH, 128), f32),
            pltpu.VMEM((Y * 128, 4 * BATCH), bf16),
            pltpu.VMEM((NODE, ROW * 128), bf16),
            pltpu.VMEM((2, WIDTH, 256), bf16),
            pltpu.VMEM((Y, ROW, 16, 128), bf16), pltpu.VMEM((ROW, Y, 16, 128), bf16),
            pltpu.VMEM((ROW, Y, 16, 128), bf16),
            dma((ROW,)), dma((ROW,)), dma((Y,)), dma((Y,)),
            pltpu.VMEM((2, 2 * BATCH, 256), bf16), pltpu.VMEM((3, 2 * BATCH, WIDTH), bf16),
            dma((4,)), dma((4,)),
            pltpu.VMEM((3, 192, WIDTH), bf16), pltpu.VMEM((3, X, 64, WIDTH), bf16), dma((3, X)), dma((3, X)),
            pltpu.VMEM((3, Y, 16, 256), bf16), pltpu.VMEM((3, Y, 16, 256), bf16), dma((3, Y)), dma((3, Y)),
            pltpu.VMEM((3, Z, 16, 256), bf16), dma((3, Z)), dma((3, Z)),
        ],
        compiler_params=pltpu.CompilerParams(
            collective_id=0, has_side_effects=True, vmem_limit_bytes=60 * 2**20
        ),
        cost_estimate=pl.CostEstimate(flops=4 * 10**9, bytes_accessed=6 * 10**6, transcendentals=2 * 10**6),
    )(
        batch_owner.reshape(1, BATCH), batch_row, batch_time,
        neighbour_owner.reshape(1, rows), neighbour_row, neighbour_time,
        frequency.reshape(1, WIDTH), phase_shift.reshape(1, WIDTH),
        owned, w_message, w_input, w_recur, cotangent.reshape(BATCH, WIDTH),
    )
    return (owned + change)[None], grad[0] + grad[1]


def solution(mesh):
    return jax.shard_map(
        body,
        mesh=mesh,
        in_specs=(
            P("group", "mem", None),
            P("group", "mem", None),
            P("group", "mem"),
            P("group", "mem"),
            P("group", "mem", None),
            P("group", "mem"),
            P("group", "mem"),
            P(),
            P(),
            P(),
            P(),
            P(),
            P("group", "mem", None),
        ),
        out_specs=(P("group", "mem", None), P("mem", None)),
        check_vma=False,
    )
```
